32 devices in a mesh: tensor: 4 (over y, x), dp: 2 (over core), replica: 4 (over z).
Axes of the slice: x: 2, y: 2, z: 4, core: 2. Of those that a mesh axis runs over, the one named last changes fastest.
Arguments:
- features: bfloat16 [8, 640, 8], P(('dp', 'replica'), 'tensor'), may hold values from -6 to 6
- output_grad: bfloat16 [8, 640, 28672], P(('dp', 'replica'), None, 'tensor'), may hold values from -6 to 6
- master: float32 [8, 1, 28672], P(('dp', 'replica'), None, 'tensor'), may hold values from -1.5 to 1.5
- first_moment: float32 [8, 1, 28672], P(('dp', 'replica'), None, 'tensor'), may hold values from -0.03 to 0.03
- second_moment: float32 [8, 1, 28672], P(('dp', 'replica'), None, 'tensor'), may hold values from 1e-06 to 0.0001
- owner_map: int32 [8], replicated, may hold values from 0 to 7, each once
- step_count: int32 [1], replicated, may hold values from 1 to 99
- learning_rate: float32 [1], replicated, may hold values from 0.005 to 0.05
Outputs:
- params: bfloat16 [8, 28672], P(None, 'tensor')
- new_master: float32 [8, 1, 28672], P(('dp', 'replica'), None, 'tensor')
- new_first: float32 [8, 1, 28672], P(('dp', 'replica'), None, 'tensor')
- new_second: float32 [8, 1, 28672], P(('dp', 'replica'), None, 'tensor')
- direction: float32 [8, 1, 28672], P(('dp', 'replica'), None, 'tensor')
The draws below stay inside these ranges and needn't reach their ends.
Inputs may be any that keep to these rules, and one draw needn't show every extreme that they name: `owner_map`: every rank owns exactly one block.
All inputs are finite; a program needn't handle non-finite values.
Results may differ from the reference program's by a relative error of at most 0.008.
Values may be sent and summed in bfloat16 or wider, within the bound.
No kernel may reach another device: no remote copies, remote signals or barrier semaphores. Data moves between devices by JAX's collectives and lax.ppermute only.
A program may use at most 64 MiB of HBM per device.

```python
import math
import jax
import jax.numpy as jnp
from jax import lax

FF = 28672
OWN_ROWS = 1
TOK_DEV = 640
RANKS = 8
ROWS = 8


def spiked(array, key, source, target, shards_of, factor):
    def block_of(dim):
        return (jnp.arange(array.shape[dim]) // (array.shape[dim] // shards_of)).reshape((-1,) + (1,) * (array.ndim - 1 - dim))

    near = jax.random.permutation(key, shards_of)[block_of(target)]
    other_side = (block_of(target) + shards_of // 2) % shards_of
    return jnp.where((block_of(source) == near) | (block_of(source) == other_side), factor * array, array)


def block_scale(stream_key, extent, shards, least, largest):
    factor_of = 1.0
    for position, shards_of in shards:
        steps = jax.random.uniform(jax.random.fold_in(jax.random.fold_in(stream_key, 6), position), (shards_of,), jnp.float32, least / len(shards), largest / len(shards))
        factor_of = factor_of * jnp.repeat(jnp.exp(steps), extent[position] // shards_of).reshape((-1,) + (1,) * (len(extent) - 1 - position))
    return factor_of


def noise(own_key, shape, spread, reach, pieces=(), kind=jnp.bfloat16):
    values = spread * jax.random.normal(own_key, shape, jnp.float32)
    if pieces:
        values = values * block_scale(own_key, shape, pieces, -0.22, 0.18)
    return jnp.clip(values, -reach, reach).astype(kind)


def noise_with(own_key, dims, scale, limit, shards, heavy, kind=jnp.bfloat16):
    drawn = scale * jax.random.normal(own_key, dims, jnp.float32)
    if shards:
        drawn = drawn * block_scale(own_key, dims, shards, -0.22, 0.18)
    return jnp.clip(spiked(drawn, jax.random.fold_in(own_key, 3), *heavy), -limit, limit).astype(kind)


def setup_inputs(seed: int = 0) -> dict:
    splits = jax.random.split(jax.random.key(seed), 9)
    return {
        "features": noise_with(splits[0], (RANKS, TOK_DEV, ROWS), 1.0, 6.0, ((0, 8), (1, 4)), (0, 2, 8, 2.0)),
        "output_grad": noise(splits[1], (RANKS, TOK_DEV, FF), 1.0, 6.0, ((0, 8), (2, 4))),
        "master": noise(splits[2], (RANKS, OWN_ROWS, FF), 0.25, 1.5, ((0, 8), (2, 4)), jnp.float32),
        "first_moment": noise(splits[3], (RANKS, OWN_ROWS, FF), 0.005, 0.03, ((0, 8), (2, 4)), jnp.float32),
        "second_moment": jnp.clip(jnp.exp(math.log(0.0001) - 4.6051702 * jax.random.uniform(splits[4], (RANKS, OWN_ROWS, FF), jnp.float32) ** block_scale(splits[4], (RANKS, OWN_ROWS, FF), ((0, 8), (2, 4)), -0.2, 0.2)), 9.999999974752427e-07, 0.0001),
        "owner_map": jax.random.permutation(splits[5], RANKS).astype(jnp.int32),
        "step_count": jax.random.randint(splits[6], (1,), 1, 100).astype(jnp.int32),
        "learning_rate": jnp.clip(jnp.exp(jax.random.uniform(splits[7], (1,), jnp.float32, math.log(0.005), math.log(0.05))), 0.005, 0.05),
    }


beta_first = 0.9
beta_second = 0.95
epsilon = 1e-08
decay_rate = 0.1

def adam_update(gradient, master, first_moment, second_moment, step_count, learning_rate):
    count_float = step_count[0].astype(jnp.float32)
    new_first = beta_first * first_moment + (1.0 - beta_first) * gradient
    new_second = beta_second * second_moment + (1.0 - beta_second) * gradient * gradient
    correct_first = 1.0 - jnp.power(jnp.float32(beta_first), count_float)
    correct_second = 1.0 - jnp.power(jnp.float32(beta_second), count_float)
    direction = new_first / correct_first / (jnp.sqrt(new_second / correct_second) + epsilon)
    new_master = master - learning_rate[0] * (direction + decay_rate * master)
    return (new_master, new_first, new_second, direction)

def reference(features, output_grad, master, first_moment, second_moment, owner_map, step_count, learning_rate):
    ranks = features.shape[0]
    tok_count = features.shape[1]
    rows_all = features.shape[2]
    columns = output_grad.shape[2]
    own_rows = master.shape[1]

    def accumulate(running, couple):
        activations, out_grads = couple
        partial_value = jnp.dot(activations.T, out_grads, preferred_element_type=jnp.float32)
        rounded = lax.optimization_barrier(partial_value.astype(jnp.bfloat16))
        return (running + rounded.astype(jnp.float32), None)
    running, unused = lax.scan(accumulate, jnp.zeros((rows_all, columns), jnp.float32), (features, output_grad))
    gradient = running / (ranks * tok_count)
    blocks = gradient.reshape(ranks, own_rows, columns)
    inverse = jnp.zeros((ranks,), jnp.int32).at[owner_map].set(jnp.arange(ranks, dtype=jnp.int32))
    owned_grad = jnp.take(blocks, inverse, axis=0)
    new_master, new_first, new_second, direction = adam_update(owned_grad, master, first_moment, second_moment, step_count, learning_rate)
    params = jnp.take(new_master.astype(jnp.bfloat16), owner_map, axis=0).reshape(rows_all, columns)
    return (params, new_master, new_first, new_second, direction)
```

```python
import functools
import math
import jax
import jax.numpy as jnp
from jax import lax
from jax.experimental import pallas as pl
from jax.experimental.pallas import tpu as pltpu
from jax.sharding import PartitionSpec as P

beta_first = 0.9
beta_second = 0.95
epsilon = 1e-08
decay_rate = 0.1
RANK_AXES = ("dp", "replica")
SHARED = 2


def chip_masks(chips):
    rest = [m for m in range(1, chips) if m != SHARED]
    return [(rest[i], rest[i + 1]) for i in range(0, len(rest), 2)]


def where_am_i():
    replicas = lax.axis_size("replica")
    dp = lax.axis_index("dp")
    core = lax.rem(dp, 2)
    chip = lax.div(dp, 2) * replicas + lax.axis_index("replica")
    return core, chip


def rank_of(chip, core):
    replicas = lax.axis_size("replica")
    return (lax.div(chip, replicas) * 2 + core) * replicas + lax.rem(chip, replicas)


def swap_cores(x):
    count = lax.axis_size("dp")
    return lax.ppermute(x, "dp", [(i, i ^ 1) for i in range(count)])


def swap_chips(x, mask_even, mask_odd):
    replicas = lax.axis_size("replica")
    pairs = []
    for dp in range(lax.axis_size("dp")):
        for z in range(replicas):
            chip = (dp // 2 * replicas + z) ^ (mask_odd if dp % 2 else mask_even)
            pairs.append((dp * replicas + z, (chip // replicas * 2 + dp % 2) * replicas + chip % replicas))
    return lax.ppermute(x, RANK_AXES, pairs)


def swap_tensor(x, mask):
    return lax.ppermute(x, "tensor", [(i, i ^ mask) for i in range(lax.axis_size("tensor"))])


def owners_of(row, chips, core, chip):
    half = chips - 2
    pairs = chip_masks(chips)
    mask = jnp.where(row < 2 * half + 2, SHARED, 0)
    for p, (even, odd) in enumerate(pairs):
        mine = jnp.where(core == 0, even, odd)
        theirs = jnp.where(core == 0, odd, even)
        mask = jnp.where(lax.div(row, 2) == p, mine, mask)
        mask = jnp.where(lax.div(row, 2) == p + len(pairs), theirs, mask)
    return rank_of(jnp.bitwise_xor(chip, mask), lax.rem(row, 2))


def matmul_kernel(chips, chunk, owner_ref, *refs):
    shards = len(refs) - 5
    f_refs, (g_ref, keep_ref, send_ref, keep_half_ref, send_half_ref) = refs[:shards], refs[shards:]
    rows = f_refs[0].shape[0]
    half = g_ref.shape[1] // 2
    served = keep_ref.shape[0]
    core, chip = where_am_i()
    place = lax.axis_index("tensor")
    blocks = [f_ref[...].astype(jnp.float32) for f_ref in f_refs]
    ordered = []
    for b in range(shards):
        block = blocks[b]
        for t in range(1, shards):
            block = jnp.where(place == t, blocks[b ^ t], block)
        ordered.append(block)
    features = jnp.concatenate(ordered, axis=1).astype(jnp.bfloat16)
    row = lax.broadcasted_iota(jnp.int32, (rows, rows), 0)
    pick = owners_of(row, chips, core, chip) == owner_ref[...]
    features = jnp.dot(
        pick.astype(jnp.float32).astype(jnp.bfloat16), features, preferred_element_type=jnp.float32
    ).astype(jnp.bfloat16)
    for side, half_ref in enumerate((keep_half_ref, send_half_ref)):
        base = (core if side == 0 else 1 - core) * half
        for k in range(half // chunk):
            columns = pl.ds(pl.multiple_of(base + k * chunk, chunk), chunk)
            part = jnp.dot(features, g_ref[:, columns], preferred_element_type=jnp.float32)
            part = part.astype(jnp.bfloat16).astype(jnp.float32)
            keep_ref[:, columns] = part[:served]
            send_ref[:, columns] = part[served : 2 * served].astype(jnp.bfloat16)
            half_ref[:, pl.ds(k * chunk, chunk)] = part[2 * served :].astype(half_ref.dtype)


def load_kernel(source_ref, out_ref, sem):
    copy = pltpu.make_async_copy(source_ref, out_ref, sem)
    copy.start()
    copy.wait()


def gradient_rows(core, chunk, k, side, sums_ref, other_ref, half_ref, other_half_ref, tokens):
    half = half_ref.shape[1]
    base = (core if side == 0 else 1 - core) * half
    columns = pl.ds(pl.multiple_of(base + k * chunk, chunk), chunk)
    place = pl.ds(k * chunk, chunk)
    total = sums_ref[:, columns] + other_ref[:, columns]
    total = total + (half_ref, other_half_ref)[side][:, place]
    return columns, place, total / tokens


def corrections(step_ref):
    count = jnp.full((1, 128), step_ref[0], jnp.int32).astype(jnp.float32)
    first = 1.0 - jnp.exp(count * math.log(beta_first))
    second = 1.0 - jnp.exp(count * math.log(beta_second))
    return first[:, :1], second[:, :1]


def adam(gradient, master, first_moment, second_moment, correct_first, correct_second, rate):
    new_first = beta_first * first_moment + (1.0 - beta_first) * gradient
    new_second = beta_second * second_moment + (1.0 - beta_second) * gradient * gradient
    direction = new_first / correct_first / (jnp.sqrt(new_second / correct_second) + epsilon)
    new_master = master - rate * (direction + decay_rate * master)
    return new_master, new_first, new_second, direction


def params_kernel(chunk, tokens, step_ref, rate_ref, sums_ref, sums_other_ref, half_ref, other_half_ref, *refs):
    state_refs, (params_ref, params_half_ref) = refs[:6], refs[6:]
    core, _ = where_am_i()
    corrected = corrections(step_ref)
    for side in range(2):
        for k in range(half_ref.shape[1] // chunk):
            columns, place, gradient = gradient_rows(
                core, chunk, k, side, sums_ref, sums_other_ref, half_ref, other_half_ref, tokens
            )
            state = []
            for own_ref, other_ref in zip(state_refs[:3], state_refs[3:]):
                own, other = own_ref[:, columns], other_ref[:, columns]
                low, high = jnp.where(core == 0, own, other), jnp.where(core == 0, other, own)
                state.append(jnp.concatenate([low, high], axis=0))
            value = adam(gradient, *state, *corrected, rate_ref[0])[0].astype(jnp.bfloat16)
            params_ref[:, columns] = value
            if side == 0:
                params_half_ref[:, place] = value


def state_kernel(chunk, tokens, step_ref, rate_ref, sums_ref, other_ref, half_ref, other_half_ref, *refs):
    state_refs, out_refs = refs[:3], refs[3:]
    core, _ = where_am_i()
    corrected = corrections(step_ref)
    for side in range(2):
        for k in range(half_ref.shape[1] // chunk):
            columns, _, gradient = gradient_rows(
                core, chunk, k, side, sums_ref, other_ref, half_ref, other_half_ref, tokens
            )
            gradient = jnp.where(core == 0, gradient[:1], gradient[1:])
            values = adam(gradient, *[ref[:, columns] for ref in state_refs], *corrected, rate_ref[0])
            for ref, value in zip(out_refs, values):
                ref[:, columns] = value


def order_kernel(chips, chunk, owner_ref, own_ref, near_ref, far_ref, half_ref, other_half_ref, out_ref):
    core, chip = where_am_i()
    rows = out_ref.shape[0]
    half = half_ref.shape[1]
    served = near_ref.shape[0]
    column = lax.broadcasted_iota(jnp.int32, (rows, rows), 1)
    owner = jnp.broadcast_to(owner_ref[...], (rows, rows)).T
    ranks = owners_of(column, chips, core, chip)
    flipped = owners_of(column, chips, 1 - core, chip)

    def pick(table, first, count):
        return (table == owner).astype(jnp.float32).astype(jnp.bfloat16)[:, first : first + count]

    near = pick(ranks, 0, served)
    far = pick(flipped, 0, served)
    shared = pick(ranks, 2 * served, 2)
    own = pick(ranks, 2 * served + 2, 2)
    for side in range(2):
        base = (core if side == 0 else 1 - core) * half
        for k in range(half // chunk):
            columns = pl.ds(pl.multiple_of(base + k * chunk, chunk), chunk)
            place = pl.ds(k * chunk, chunk)
            total = jnp.dot(own, own_ref[:, columns], preferred_element_type=jnp.float32)
            total += jnp.dot(near, near_ref[:, columns], preferred_element_type=jnp.float32)
            total += jnp.dot(far, far_ref[:, columns], preferred_element_type=jnp.float32)
            total += jnp.dot(
                shared, (half_ref, other_half_ref)[side][:, place], preferred_element_type=jnp.float32
            )
            out_ref[:, columns] = total.astype(jnp.bfloat16)


VMEM = pl.BlockSpec(memory_space=pltpu.VMEM)
SMEM = pl.BlockSpec(memory_space=pltpu.SMEM)


def call(kernel, outs, specs, name, limit=4 << 20):
    return pl.pallas_call(
        kernel,
        out_shape=[jax.ShapeDtypeStruct(shape, dtype) for shape, dtype in outs],
        in_specs=specs,
        out_specs=[VMEM] * len(outs),
        compiler_params=pltpu.CompilerParams(vmem_limit_bytes=limit),
        name=name,
    )


def on_device(
    features, output_grad, master, first_moment, second_moment, owner_map, step_count, learning_rate
):
    replicas = lax.axis_size("replica")
    chips = lax.axis_size("dp") // 2 * replicas
    shards = lax.axis_size("tensor")
    _, tokens, columns = output_grad.shape
    rows = features.shape[2]
    ranks = owner_map.shape[0]
    half = columns // 2
    served = chips - 2
    chunk = 512 if half % 512 == 0 else 128
    pairs = chip_masks(chips)
    f32, bf16 = jnp.float32, jnp.bfloat16

    mine = features[0].T
    blocks = [mine] + [swap_tensor(mine, t) for t in range(1, shards)]
    state = [x.reshape(1, columns) for x in (master, first_moment, second_moment)]
    partner = [swap_cores(x) for x in state]
    owners = owner_map.reshape(1, ranks)

    loaded = pl.pallas_call(
        load_kernel,
        out_shape=jax.ShapeDtypeStruct((tokens, columns), bf16),
        in_specs=[pl.BlockSpec(memory_space=pl.ANY)],
        out_specs=VMEM,
        scratch_shapes=[pltpu.SemaphoreType.DMA],
        compiler_params=pltpu.CompilerParams(vmem_limit_bytes=4 << 20),
        cost_estimate=pl.CostEstimate(
            flops=0, bytes_accessed=4 * tokens * columns, transcendentals=0
        ),
        name="load_output_grad",
    )(output_grad[0])
    keep, send, keep_half, send_half = call(
        functools.partial(matmul_kernel, chips, chunk),
        [((served, columns), f32), ((served, columns), bf16), ((4, half), f32), ((4, half), bf16)],
        [VMEM] * (shards + 2),
        "partial_gradient",
    )(owners, *blocks, loaded)
    sums = (keep + swap_cores(send).astype(f32)).astype(bf16)
    sums_half = keep_half + swap_cores(send_half).astype(f32)
    arrived = [swap_chips(sums[2 * p : 2 * p + 2], *pair) for p, pair in enumerate(pairs)]
    arrived_half = swap_chips(sums_half[:2].astype(bf16), SHARED, SHARED)
    row_sums = sum(x.astype(f32) for x in arrived)
    row_half = arrived_half.astype(f32) + sums_half[2:]
    grads = (row_sums, swap_cores(row_sums), row_half, swap_cores(row_half))

    total = float(tokens * ranks)
    params, params_half = call(
        functools.partial(params_kernel, chunk, total),
        [((2, columns), bf16), ((2, half), bf16)],
        [SMEM, SMEM] + [VMEM] * 10,
        "chip_params",
    )(step_count, learning_rate, *grads, *state, *partner)
    outs = call(
        functools.partial(state_kernel, chunk, total),
        [((1, columns), f32)] * 4,
        [SMEM, SMEM] + [VMEM] * 7,
        "own_state",
    )(step_count, learning_rate, *grads, *state)
    near = jnp.concatenate([swap_chips(params, *pair) for pair in pairs], axis=0)
    near_half = swap_chips(params_half, SHARED, SHARED)
    ordered = call(
        functools.partial(order_kernel, chips, chunk),
        [((rows, columns), bf16)],
        [VMEM] * 6,
        "row_order",
    )(owners, params, near, swap_cores(near), near_half, swap_cores(near_half))
    return (ordered[0], *[x.reshape(master.shape) for x in outs])


def solution(mesh):
    in_specs = (
        P(("dp", "replica"), "tensor", None),
        P(("dp", "replica"), None, "tensor"),
        P(("dp", "replica"), None, "tensor"),
        P(("dp", "replica"), None, "tensor"),
        P(("dp", "replica"), None, "tensor"),
        P(),
        P(),
        P(),
    )
    out_specs = (
        P(None, "tensor"),
        P(("dp", "replica"), None, "tensor"),
        P(("dp", "replica"), None, "tensor"),
        P(("dp", "replica"), None, "tensor"),
        P(("dp", "replica"), None, "tensor"),
    )
    return jax.shard_map(
        on_device, mesh=mesh, in_specs=in_specs, out_specs=out_specs, check_vma=False
    )
```

```python
import functools
import math
import jax
import jax.numpy as jnp
from jax import lax
from jax.experimental import pallas as pl
from jax.experimental.pallas import tpu as pltpu
from jax.sharding import PartitionSpec as P

beta_first = 0.9
beta_second = 0.95
epsilon = 1e-08
decay_rate = 0.1
f32, bf16 = jnp.float32, jnp.bfloat16
RANK_AXES = ("dp", "replica")
SHARED = 1


def chip_masks(chips):
    rest = [m for m in range(1, chips) if m != SHARED]
    return [(rest[i], rest[i + 1]) for i in range(0, len(rest), 2)]


def where_am_i():
    replicas = lax.axis_size("replica")
    dp = lax.axis_index("dp")
    core = lax.rem(dp, 2)
    chip = lax.div(dp, 2) * replicas + lax.axis_index("replica")
    return core, chip


def rank_of(chip, core):
    replicas = lax.axis_size("replica")
    return (lax.div(chip, replicas) * 2 + core) * replicas + lax.rem(chip, replicas)


def swap_cores(x):
    count = lax.axis_size("dp")
    return lax.ppermute(x, "dp", [(i, i ^ 1) for i in range(count)])


def swap_chips(x, mask_even, mask_odd):
    replicas = lax.axis_size("replica")
    pairs = []
    for dp in range(lax.axis_size("dp")):
        for z in range(replicas):
            chip = (dp // 2 * replicas + z) ^ (mask_odd if dp % 2 else mask_even)
            pairs.append((dp * replicas + z, (chip // replicas * 2 + dp % 2) * replicas + chip % replicas))
    return lax.ppermute(x, RANK_AXES, pairs)


def swap_tensor(x, mask):
    return lax.ppermute(x, "tensor", [(i, i ^ mask) for i in range(lax.axis_size("tensor"))])


def owners_of(row, chips, core, chip):
    half = chips - 2
    pairs = chip_masks(chips)
    mask = jnp.where(row < 2 * half + 2, SHARED, 0)
    for p, (even, odd) in enumerate(pairs):
        mine = jnp.where(core == 0, even, odd)
        theirs = jnp.where(core == 0, odd, even)
        mask = jnp.where(lax.div(row, 2) == p, mine, mask)
        mask = jnp.where(lax.div(row, 2) == p + len(pairs), theirs, mask)
    return rank_of(jnp.bitwise_xor(chip, mask), lax.rem(row, 2))


def halves(core, half, chunk, k):
    mine = pl.ds(pl.multiple_of(core * half + k * chunk, chunk), chunk)
    other = pl.ds(pl.multiple_of((1 - core) * half + k * chunk, chunk), chunk)
    return mine, other, pl.ds(k * chunk, chunk)


def owners_kernel(chips, out_ref):
    core, chip = where_am_i()
    out_ref[...] = owners_of(lax.broadcasted_iota(jnp.int32, out_ref.shape, 0), chips, core, chip)


def ordered(table_ref, owner_ref, features):
    pick = (table_ref[...] == owner_ref[...]).astype(f32).astype(bf16)
    return jnp.dot(pick, features.astype(bf16), preferred_element_type=f32).astype(bf16)


def token_rows(depth, mask, count=1):
    first = jnp.bitwise_xor(lax.axis_index("tensor"), mask)
    if count > 1:
        first = first - lax.rem(first, count)
    return pl.ds(pl.multiple_of(first * depth, 32), count * depth)


def own_kernel(chunk, table_ref, owner_ref, feature_ref, g_ref, *refs):
    (total_ref,) = refs
    features = ordered(table_ref, owner_ref, feature_ref[...])
    held = token_rows(feature_ref.shape[1], 0)
    for k in range(total_ref.shape[1] // chunk):
        columns = pl.ds(k * chunk, chunk)
        total_ref[:, columns] = jnp.dot(features, g_ref[held, columns], preferred_element_type=f32)


def pair_kernel(chunk, table_ref, owner_ref, even_ref, odd_ref, g_ref, before_ref, total_ref):
    low = lax.rem(lax.axis_index("tensor"), 2)
    even, odd = even_ref[...].astype(f32), odd_ref[...].astype(f32)
    blocks = [jnp.where(low == 0, even, odd), jnp.where(low == 0, odd, even)]
    features = ordered(table_ref, owner_ref, jnp.concatenate(blocks, axis=1))
    held = token_rows(even_ref.shape[1], 2, 2)
    for k in range(total_ref.shape[1] // chunk):
        columns = pl.ds(k * chunk, chunk)
        part = jnp.dot(features, g_ref[held, columns], preferred_element_type=f32)
        total_ref[:, columns] = before_ref[:, columns] + part


def last_kernel(chips, chunk, table_ref, owner_ref, feature_ref, g_ref, before_ref, *refs):
    own_refs, partner_refs, (keep_ref, send_ref, *state_refs) = refs[:3], refs[3:6], refs[6:]
    features = ordered(table_ref, owner_ref, feature_ref[...])
    held = token_rows(feature_ref.shape[1], 1)
    half = keep_ref.shape[1]
    served = chips - 2
    core, _ = where_am_i()
    for k in range(half // chunk):
        *sides, place = halves(core, half, chunk, k)
        mine, other = [
            (jnp.dot(features, g_ref[held, columns], preferred_element_type=f32) + before_ref[:, columns])
            .astype(bf16)
            .astype(f32)
            for columns in sides
        ]
        keep, send = [], []
        for p in range(0, served, 2):
            keep += [other[p : p + 2], mine[p : p + 2]]
            send += [mine[served + p : served + p + 2], other[served + p : served + p + 2]]
        keep_ref[:, place] = jnp.concatenate(keep + [mine[2 * served :]], axis=0)
        send_ref[:, place] = jnp.concatenate(send + [other[2 * served :]], axis=0).astype(bf16)
    for own_ref, partner_ref, ref in zip(own_refs, partner_refs, state_refs):
        own, partner = own_ref[...], partner_ref[...]
        ref[:1] = jnp.where(core == 0, own, partner)
        ref[1:] = jnp.where(core == 0, partner, own)


def corrections(step_ref):
    count = jnp.full((1, 128), step_ref[0], jnp.int32).astype(f32)
    first = 1.0 - jnp.exp(count * math.log(beta_first))
    second = 1.0 - jnp.exp(count * math.log(beta_second))
    return first[:, :1], second[:, :1]


def adam(gradient, master, first_moment, second_moment, correct_first, correct_second, rate):
    new_first = beta_first * first_moment + (1.0 - beta_first) * gradient
    new_second = beta_second * second_moment + (1.0 - beta_second) * gradient * gradient
    direction = new_first / correct_first / (jnp.sqrt(new_second / correct_second) + epsilon)
    new_master = master - rate * (direction + decay_rate * master)
    return new_master, new_first, new_second, direction


def chip_gradients(sums, others, tokens):
    return (sums[2:] + others[:2]) / tokens, (sums[:2] + others[2:]) / tokens


def params_kernel(chunk, tokens, step_ref, rate_ref, sums_ref, others_ref, *refs):
    state_refs, (params_ref, params_half_ref) = refs[:3], refs[3:]
    core, _ = where_am_i()
    corrected = corrections(step_ref)
    half = sums_ref.shape[1]
    for k in range(half // chunk):
        *sides, place = halves(core, half, chunk, k)
        values = []
        for columns, gradient in zip(sides, chip_gradients(sums_ref[:, place], others_ref[:, place], tokens)):
            state = [ref[:, columns] for ref in state_refs]
            values.append(adam(gradient, *state, *corrected, rate_ref[0])[0])
        params_ref[:, place] = jnp.concatenate(values[::-1], axis=0).astype(bf16)
        params_half_ref[:, place] = values[0].astype(bf16)


def state_kernel(chunk, tokens, step_ref, rate_ref, sums_ref, others_ref, *refs):
    state_refs, out_refs = refs[:3], refs[3:]
    core, _ = where_am_i()
    corrected = corrections(step_ref)
    half = sums_ref.shape[1]
    for k in range(half // chunk):
        *sides, place = halves(core, half, chunk, k)
        for columns, gradient in zip(sides, chip_gradients(sums_ref[:, place], others_ref[:, place], tokens)):
            gradient = jnp.where(core == 0, gradient[:1], gradient[1:])
            values = adam(gradient, *[ref[:, columns] for ref in state_refs], *corrected, rate_ref[0])
            for ref, value in zip(out_refs, values):
                ref[:, columns] = value


def picker(chips, rows, owner_ref, core, chip):
    column = lax.broadcasted_iota(jnp.int32, (rows, rows), 0)
    hot = (owners_of(column, chips, core, chip) == owner_ref[...]).astype(f32).T
    return hot.astype(bf16)


def early_kernel(chips, chunk, owner_ref, own_ref, half_ref, *refs):
    near_refs, total_ref = refs[:-1], refs[-1]
    core, chip = where_am_i()
    half = half_ref.shape[1]
    served = chips - 2
    pick = picker(chips, total_ref.shape[0], owner_ref, core, chip)
    own = pick[:, 2 * served + 2 :]
    shared = pick[:, 2 * served : 2 * served + 2]
    for k in range(half // chunk):
        mine, other, place = halves(core, half, chunk, k)
        rows = own_ref[:, place].astype(f32)
        total = jnp.dot(shared, half_ref[:, place], preferred_element_type=f32)
        total += jnp.dot(own, rows[2:].astype(bf16), preferred_element_type=f32)
        total_other = jnp.dot(own, rows[:2].astype(bf16), preferred_element_type=f32)
        for p, near_ref in enumerate(near_refs):
            near = pick[:, 2 * p : 2 * p + 2]
            rows = near_ref[:, place].astype(f32)
            total += jnp.dot(near, rows[2:].astype(bf16), preferred_element_type=f32)
            total_other += jnp.dot(near, rows[:2].astype(bf16), preferred_element_type=f32)
        total_ref[:, mine] = total
        total_ref[:, other] = total_other


def order_kernel(chips, chunk, owner_ref, total_ref, half_ref, *refs):
    far_refs, out_ref = refs[:-1], refs[-1]
    core, chip = where_am_i()
    half = half_ref.shape[1]
    served = chips - 2
    pick = picker(chips, total_ref.shape[0], owner_ref, core, chip)
    shared = pick[:, 2 * served : 2 * served + 2]
    for k in range(half // chunk):
        mine, other, place = halves(core, half, chunk, k)
        total = total_ref[:, mine]
        total_other = total_ref[:, other] + jnp.dot(shared, half_ref[:, place], preferred_element_type=f32)
        for p, far_ref in enumerate(far_refs):
            far = pick[:, served + 2 * p : served + 2 * p + 2]
            rows = far_ref[:, place].astype(f32)
            total += jnp.dot(far, rows[:2].astype(bf16), preferred_element_type=f32)
            total_other += jnp.dot(far, rows[2:].astype(bf16), preferred_element_type=f32)
        out_ref[:, mine] = total.astype(bf16)
        out_ref[:, other] = total_other.astype(bf16)


VMEM = pl.BlockSpec(memory_space=pltpu.VMEM)
SMEM = pl.BlockSpec(memory_space=pltpu.SMEM)


def call(kernel, outs, specs, name, cost=None):
    return pl.pallas_call(
        kernel,
        out_shape=[jax.ShapeDtypeStruct(shape, dtype) for shape, dtype in outs],
        in_specs=specs,
        out_specs=[VMEM] * len(outs),
        compiler_params=pltpu.CompilerParams(vmem_limit_bytes=4 << 20),
        cost_estimate=cost,
        name=name,
    )


def on_device(
    features, output_grad, master, first_moment, second_moment, owner_map, step_count, learning_rate
):
    replicas = lax.axis_size("replica")
    chips = lax.axis_size("dp") // 2 * replicas
    _, tokens, columns = output_grad.shape
    rows = features.shape[2]
    ranks = owner_map.shape[0]
    half = columns // 2
    served = chips - 2
    chunk = 512 if half % 512 == 0 else 128
    pairs = chip_masks(chips)
    source = output_grad[0]
    owners = owner_map.reshape(1, ranks)

    mine = features[0].T
    diagonal, next_two, next_one = [swap_tensor(mine, mask) for mask in (3, 2, 1)]
    state = [x.reshape(1, columns) for x in (master, first_moment, second_moment)]
    (table,) = call(
        functools.partial(owners_kernel, chips),
        [((rows, rows), jnp.int32)],
        [],
        "owners",
        pl.CostEstimate(flops=3_500_000_000, bytes_accessed=0, transcendentals=0),
    )()
    total = ((rows, columns), f32)
    (part,) = call(functools.partial(own_kernel, chunk), [total], [VMEM] * 4, "own_tokens")(
        table, owners, mine, source
    )
    partner = [swap_cores(x) for x in state]
    (part,) = call(functools.partial(pair_kernel, chunk), [total], [VMEM] * 6, "pair_tokens")(
        table, owners, next_two, diagonal, source, part
    )
    keep, send, *state_rows = call(
        functools.partial(last_kernel, chips, chunk),
        [((2 * served + 4, half), f32), ((2 * served + 4, half), bf16)] + [((2, columns), f32)] * 3,
        [VMEM] * 11,
        "last_tokens",
    )(table, owners, next_one, source, part, *state, *partner)

    sums = keep + swap_cores(send).astype(f32)
    arrived = [swap_chips(sums[4 * p : 4 * p + 4].astype(bf16), *pair) for p, pair in enumerate(pairs)]
    arrived_half = swap_chips(sums[2 * served : 2 * served + 2].astype(bf16), SHARED, SHARED)
    sums_half = arrived_half.astype(f32) + sums[2 * served + 2 :]
    arrived = sum(x.astype(f32) for x in arrived)
    chip_sums = jnp.concatenate([arrived[:2], arrived[2:] + sums_half], axis=0)
    grads = (chip_sums, swap_cores(chip_sums))

    count = float(tokens * ranks)
    params, params_half = call(
        functools.partial(params_kernel, chunk, count),
        [((4, half), bf16), ((2, half), bf16)],
        [SMEM, SMEM] + [VMEM] * 5,
        "chip_params",
    )(step_count, learning_rate, *grads, *state_rows)
    outs = call(
        functools.partial(state_kernel, chunk, count),
        [((1, columns), f32)] * 4,
        [SMEM, SMEM] + [VMEM] * 5,
        "own_state",
    )(step_count, learning_rate, *grads, *state)
    near = [swap_chips(params, *pair) for pair in pairs]
    near_half = swap_chips(params_half, SHARED, SHARED)
    far = [swap_cores(x) for x in near]
    far_half = swap_cores(near_half)
    (early,) = call(
        functools.partial(early_kernel, chips, chunk), [total], [VMEM] * (3 + len(near)), "early_rows"
    )(owners, params, near_half, *near)
    (params,) = call(
        functools.partial(order_kernel, chips, chunk),
        [((rows, columns), bf16)],
        [VMEM] * (3 + len(far)),
        "row_order",
    )(owners, early, far_half, *far)
    return (params, *[x.reshape(master.shape) for x in outs])


def solution(mesh):
    in_specs = (
        P(("dp", "replica"), "tensor", None),
        P(("dp", "replica"), None, "tensor"),
        P(("dp", "replica"), None, "tensor"),
        P(("dp", "replica"), None, "tensor"),
        P(("dp", "replica"), None, "tensor"),
        P(),
        P(),
        P(),
    )
    out_specs = (
        P(None, "tensor"),
        P(("dp", "replica"), None, "tensor"),
        P(("dp", "replica"), None, "tensor"),
        P(("dp", "replica"), None, "tensor"),
        P(("dp", "replica"), None, "tensor"),
    )
    return jax.shard_map(
        on_device, mesh=mesh, in_specs=in_specs, out_specs=out_specs, check_vma=False
    )
```

```python
import functools
import math
import jax
import jax.numpy as jnp
from jax import lax
from jax.experimental import pallas as pl
from jax.experimental.pallas import tpu as pltpu
from jax.sharding import PartitionSpec as P

beta_first = 0.9
beta_second = 0.95
epsilon = 1e-08
decay_rate = 0.1
f32, bf16 = jnp.float32, jnp.bfloat16
RANK_AXES = ("dp", "replica")
SHARED = 1


def chip_masks(chips):
    rest = [m for m in range(1, chips) if m != SHARED]
    return [(rest[i], rest[i + 1]) for i in range(0, len(rest), 2)]


def where_am_i():
    replicas = lax.axis_size("replica")
    dp = lax.axis_index("dp")
    core = lax.rem(dp, 2)
    chip = lax.div(dp, 2) * replicas + lax.axis_index("replica")
    return core, chip


def rank_of(chip, core):
    replicas = lax.axis_size("replica")
    return (lax.div(chip, replicas) * 2 + core) * replicas + lax.rem(chip, replicas)


def swap_cores(x):
    count = lax.axis_size("dp")
    return lax.ppermute(x, "dp", [(i, i ^ 1) for i in range(count)])


def swap_chips(x, mask_even, mask_odd):
    replicas = lax.axis_size("replica")
    pairs = []
    for dp in range(lax.axis_size("dp")):
        for z in range(replicas):
            chip = (dp // 2 * replicas + z) ^ (mask_odd if dp % 2 else mask_even)
            pairs.append((dp * replicas + z, (chip // replicas * 2 + dp % 2) * replicas + chip % replicas))
    return lax.ppermute(x, RANK_AXES, pairs)


def swap_tensor(x, mask):
    return lax.ppermute(x, "tensor", [(i, i ^ mask) for i in range(lax.axis_size("tensor"))])


def owners_of(row, chips, core, chip):
    half = chips - 2
    pairs = chip_masks(chips)
    mask = jnp.where(row < 2 * half + 2, SHARED, 0)
    for p, (even, odd) in enumerate(pairs):
        mine = jnp.where(core == 0, even, odd)
        theirs = jnp.where(core == 0, odd, even)
        mask = jnp.where(lax.div(row, 2) == p, mine, mask)
        mask = jnp.where(lax.div(row, 2) == p + len(pairs), theirs, mask)
    return rank_of(jnp.bitwise_xor(chip, mask), lax.rem(row, 2))


def halves(core, half, chunk, k):
    mine = pl.ds(pl.multiple_of(core * half + k * chunk, chunk), chunk)
    other = pl.ds(pl.multiple_of((1 - core) * half + k * chunk, chunk), chunk)
    return mine, other, pl.ds(k * chunk, chunk)


def owners_kernel(chips, out_ref):
    core, chip = where_am_i()
    out_ref[...] = owners_of(lax.broadcasted_iota(jnp.int32, out_ref.shape, 0), chips, core, chip)


def ordered(table_ref, owner_ref, features):
    pick = (table_ref[...] == owner_ref[...]).astype(f32).astype(bf16)
    return jnp.dot(pick, features.astype(bf16), preferred_element_type=f32).astype(bf16)


def token_rows(depth, mask):
    shard = jnp.bitwise_xor(lax.axis_index("tensor"), mask)
    return pl.ds(pl.multiple_of(shard * depth, 32), depth)


def own_kernel(chunk, table_ref, owner_ref, feature_ref, g_ref, *refs):
    (total_ref,) = refs
    features = ordered(table_ref, owner_ref, feature_ref[...])
    held = token_rows(feature_ref.shape[1], 0)
    for k in range(total_ref.shape[1] // chunk):
        columns = pl.ds(k * chunk, chunk)
        total_ref[:, columns] = jnp.dot(features, g_ref[held, columns], preferred_element_type=f32)


def add_kernel(chunk, mask, table_ref, owner_ref, feature_ref, g_ref, before_ref, total_ref):
    features = ordered(table_ref, owner_ref, feature_ref[...])
    held = token_rows(feature_ref.shape[1], mask)
    for k in range(total_ref.shape[1] // chunk):
        columns = pl.ds(k * chunk, chunk)
        part = jnp.dot(features, g_ref[held, columns], preferred_element_type=f32)
        total_ref[:, columns] = before_ref[:, columns] + part


def last_kernel(chips, chunk, table_ref, owner_ref, feature_ref, g_ref, before_ref, *refs):
    own_refs, partner_refs, (keep_ref, send_ref, *state_refs) = refs[:3], refs[3:6], refs[6:]
    features = ordered(table_ref, owner_ref, feature_ref[...])
    held = token_rows(feature_ref.shape[1], 1)
    half = keep_ref.shape[1]
    served = chips - 2
    core, _ = where_am_i()
    for k in range(half // chunk):
        *sides, place = halves(core, half, chunk, k)
        mine, other = [
            (jnp.dot(features, g_ref[held, columns], preferred_element_type=f32) + before_ref[:, columns])
            .astype(bf16)
            .astype(f32)
            for columns in sides
        ]
        keep, send = [], []
        for p in range(0, served, 2):
            keep += [other[p : p + 2], mine[p : p + 2]]
            send += [mine[served + p : served + p + 2], other[served + p : served + p + 2]]
        keep_ref[:, place] = jnp.concatenate(keep + [mine[2 * served :]], axis=0)
        send_ref[:, place] = jnp.concatenate(send + [other[2 * served :]], axis=0).astype(bf16)
    for own_ref, partner_ref, ref in zip(own_refs, partner_refs, state_refs):
        own, partner = own_ref[...], partner_ref[...]
        ref[:1] = jnp.where(core == 0, own, partner)
        ref[1:] = jnp.where(core == 0, partner, own)


def corrections(step_ref):
    count = jnp.full((1, 128), step_ref[0], jnp.int32).astype(f32)
    first = 1.0 - jnp.exp(count * math.log(beta_first))
    second = 1.0 - jnp.exp(count * math.log(beta_second))
    return first[:, :1], second[:, :1]


def adam(gradient, master, first_moment, second_moment, correct_first, correct_second, rate):
    new_first = beta_first * first_moment + (1.0 - beta_first) * gradient
    new_second = beta_second * second_moment + (1.0 - beta_second) * gradient * gradient
    direction = new_first / correct_first / (jnp.sqrt(new_second / correct_second) + epsilon)
    new_master = master - rate * (direction + decay_rate * master)
    return new_master, new_first, new_second, direction


def chip_gradients(sums, others, tokens):
    return (sums[2:] + others[:2]) / tokens, (sums[:2] + others[2:]) / tokens


def params_kernel(chunk, tokens, step_ref, rate_ref, sums_ref, others_ref, *refs):
    state_refs, (params_ref, params_half_ref) = refs[:3], refs[3:]
    core, _ = where_am_i()
    corrected = corrections(step_ref)
    half = sums_ref.shape[1]
    for k in range(half // chunk):
        *sides, place = halves(core, half, chunk, k)
        values = []
        for columns, gradient in zip(sides, chip_gradients(sums_ref[:, place], others_ref[:, place], tokens)):
            state = [ref[:, columns] for ref in state_refs]
            values.append(adam(gradient, *state, *corrected, rate_ref[0])[0])
        params_ref[:, place] = jnp.concatenate(values[::-1], axis=0).astype(bf16)
        params_half_ref[:, place] = values[0].astype(bf16)


def state_kernel(chunk, tokens, step_ref, rate_ref, sums_ref, others_ref, *refs):
    state_refs, out_refs = refs[:3], refs[3:]
    core, _ = where_am_i()
    corrected = corrections(step_ref)
    half = sums_ref.shape[1]
    for k in range(half // chunk):
        *sides, place = halves(core, half, chunk, k)
        for columns, gradient in zip(sides, chip_gradients(sums_ref[:, place], others_ref[:, place], tokens)):
            gradient = jnp.where(core == 0, gradient[:1], gradient[1:])
            values = adam(gradient, *[ref[:, columns] for ref in state_refs], *corrected, rate_ref[0])
            for ref, value in zip(out_refs, values):
                ref[:, columns] = value


def picker(chips, rows, owner_ref, core, chip):
    column = lax.broadcasted_iota(jnp.int32, (rows, rows), 0)
    hot = (owners_of(column, chips, core, chip) == owner_ref[...]).astype(f32).T
    return hot.astype(bf16)


def early_kernel(chips, chunk, owner_ref, own_ref, half_ref, *refs):
    near_refs, (total_ref, pick_ref) = refs[:-2], refs[-2:]
    core, chip = where_am_i()
    half = half_ref.shape[1]
    served = chips - 2
    pick = picker(chips, total_ref.shape[0], owner_ref, core, chip)
    pick_ref[...] = pick
    own = pick[:, 2 * served + 2 :]
    shared = pick[:, 2 * served : 2 * served + 2]
    for k in range(half // chunk):
        mine, other, place = halves(core, half, chunk, k)
        rows = own_ref[:, place].astype(f32)
        total = jnp.dot(shared, half_ref[:, place], preferred_element_type=f32)
        total += jnp.dot(own, rows[2:].astype(bf16), preferred_element_type=f32)
        total_other = jnp.dot(own, rows[:2].astype(bf16), preferred_element_type=f32)
        for p, near_ref in enumerate(near_refs):
            near = pick[:, 2 * p : 2 * p + 2]
            rows = near_ref[:, place].astype(f32)
            total += jnp.dot(near, rows[2:].astype(bf16), preferred_element_type=f32)
            total_other += jnp.dot(near, rows[:2].astype(bf16), preferred_element_type=f32)
        total_ref[:, mine] = total
        total_ref[:, other] = total_other


def order_kernel(chips, chunk, pick_ref, total_ref, far_ref, out_ref, rows_ref, sems):
    core, _ = where_am_i()
    half = far_ref.shape[1]
    served = chips - 2
    pick = pick_ref[...]
    shared = pick[:, 2 * served : 2 * served + 2]
    copies = []
    for side in range(2):
        for k in range(half // chunk):
            *sides, place = halves(core, half, chunk, k)
            rows = far_ref[:, place].astype(f32)
            total = total_ref[:, sides[side]]
            if side:
                total += jnp.dot(shared, rows[:2].astype(bf16), preferred_element_type=f32)
            for p in range(served // 2):
                far = pick[:, served + 2 * p : served + 2 * p + 2]
                first = 4 * p + (4 if side else 2)
                total += jnp.dot(far, rows[first : first + 2].astype(bf16), preferred_element_type=f32)
            rows_ref[:, sides[side]] = total.astype(bf16)
        done = halves(core, half, half, 0)[side]
        copies.append(pltpu.make_async_copy(rows_ref.at[:, done], out_ref.at[:, done], sems.at[side]))
        copies[side].start()
    for copy in copies:
        copy.wait()


VMEM = pl.BlockSpec(memory_space=pltpu.VMEM)
SMEM = pl.BlockSpec(memory_space=pltpu.SMEM)


def call(kernel, outs, specs, name, cost=None, out_spec=VMEM, scratch=()):
    return pl.pallas_call(
        kernel,
        out_shape=[jax.ShapeDtypeStruct(shape, dtype) for shape, dtype in outs],
        in_specs=specs,
        out_specs=[out_spec] * len(outs),
        scratch_shapes=scratch,
        compiler_params=pltpu.CompilerParams(vmem_limit_bytes=4 << 20),
        cost_estimate=cost,
        name=name,
    )


def on_device(
    features, output_grad, master, first_moment, second_moment, owner_map, step_count, learning_rate
):
    replicas = lax.axis_size("replica")
    chips = lax.axis_size("dp") // 2 * replicas
    _, tokens, columns = output_grad.shape
    rows = features.shape[2]
    ranks = owner_map.shape[0]
    half = columns // 2
    served = chips - 2
    chunk = 512 if half % 512 == 0 else 128
    pairs = chip_masks(chips)
    source = output_grad[0]
    owners = owner_map.reshape(1, ranks)

    mine = features[0].T
    diagonal, next_two, next_one = [swap_tensor(mine, mask) for mask in (3, 2, 1)]
    state = [x.reshape(1, columns) for x in (master, first_moment, second_moment)]
    (table,) = call(
        functools.partial(owners_kernel, chips),
        [((rows, rows), jnp.int32)],
        [],
        "owners",
        pl.CostEstimate(flops=3_000_000_000, bytes_accessed=0, transcendentals=0),
    )()
    total = ((rows, columns), f32)
    (part,) = call(functools.partial(own_kernel, chunk), [total], [VMEM] * 4, "own_tokens")(
        table, owners, mine, source
    )
    partner = [swap_cores(x) for x in state]
    for mask, block, name in ((3, diagonal, "diagonal_tokens"), (2, next_two, "next_two_tokens")):
        (part,) = call(functools.partial(add_kernel, chunk, mask), [total], [VMEM] * 5, name)(
            table, owners, block, source, part
        )
    keep, send, *state_rows = call(
        functools.partial(last_kernel, chips, chunk),
        [((2 * served + 4, half), f32), ((2 * served + 4, half), bf16)] + [((2, columns), f32)] * 3,
        [VMEM] * 11,
        "last_tokens",
    )(table, owners, next_one, source, part, *state, *partner)

    sums = keep + swap_cores(send).astype(f32)
    arrived = [swap_chips(sums[4 * p : 4 * p + 4].astype(bf16), *pair) for p, pair in enumerate(pairs)]
    arrived_half = swap_chips(sums[2 * served : 2 * served + 2].astype(bf16), SHARED, SHARED)
    sums_half = arrived_half.astype(f32) + sums[2 * served + 2 :]
    arrived = sum(x.astype(f32) for x in arrived)
    chip_sums = jnp.concatenate([arrived[:2], arrived[2:] + sums_half], axis=0)
    grads = (chip_sums, swap_cores(chip_sums))

    count = float(tokens * ranks)
    params, params_half = call(
        functools.partial(params_kernel, chunk, count),
        [((4, half), bf16), ((2, half), bf16)],
        [SMEM, SMEM] + [VMEM] * 5,
        "chip_params",
    )(step_count, learning_rate, *grads, *state_rows)
    outs = call(
        functools.partial(state_kernel, chunk, count),
        [((1, columns), f32)] * 4,
        [SMEM, SMEM] + [VMEM] * 5,
        "own_state",
    )(step_count, learning_rate, *grads, *state)
    near = [swap_chips(params, *pair) for pair in pairs]
    near_half = swap_chips(params_half, SHARED, SHARED)
    far = swap_cores(jnp.concatenate([near_half, *near], axis=0))
    early, pick = call(
        functools.partial(early_kernel, chips, chunk),
        [total, ((rows, rows), bf16)],
        [VMEM] * (3 + len(near)),
        "early_rows",
        pl.CostEstimate(flops=5_000_000_000, bytes_accessed=0, transcendentals=0),
    )(owners, params, near_half, *near)
    (params,) = call(
        functools.partial(order_kernel, chips, chunk),
        [((rows, columns), bf16)],
        [VMEM] * 3,
        "row_order",
        out_spec=pl.BlockSpec(memory_space=pl.ANY),
        scratch=[pltpu.VMEM((rows, columns), bf16), pltpu.SemaphoreType.DMA((2,))],
    )(pick, early, far)
    return (params, *[x.reshape(master.shape) for x in outs])


def solution(mesh):
    in_specs = (
        P(("dp", "replica"), "tensor", None),
        P(("dp", "replica"), None, "tensor"),
        P(("dp", "replica"), None, "tensor"),
        P(("dp", "replica"), None, "tensor"),
        P(("dp", "replica"), None, "tensor"),
        P(),
        P(),
        P(),
    )
    out_specs = (
        P(None, "tensor"),
        P(("dp", "replica"), None, "tensor"),
        P(("dp", "replica"), None, "tensor"),
        P(("dp", "replica"), None, "tensor"),
        P(("dp", "replica"), None, "tensor"),
    )
    return jax.shard_map(
        on_device, mesh=mesh, in_specs=in_specs, out_specs=out_specs, check_vma=False
    )
```

```python
import functools
import math
import jax
import jax.numpy as jnp
from jax import lax
from jax.experimental import pallas as pl
from jax.experimental.pallas import tpu as pltpu
from jax.sharding import PartitionSpec as P

beta_first = 0.9
beta_second = 0.95
epsilon = 1e-08
decay_rate = 0.1
f32, bf16 = jnp.float32, jnp.bfloat16
RANK_AXES = ("dp", "replica")
SHARED = 1


def chip_masks(chips):
    rest = [m for m in range(1, chips) if m != SHARED]
    return [(rest[i], rest[i + 1]) for i in range(0, len(rest), 2)]


def where_am_i():
    replicas = lax.axis_size("replica")
    dp = lax.axis_index("dp")
    core = lax.rem(dp, 2)
    chip = lax.div(dp, 2) * replicas + lax.axis_index("replica")
    return core, chip


def rank_of(chip, core):
    replicas = lax.axis_size("replica")
    return (lax.div(chip, replicas) * 2 + core) * replicas + lax.rem(chip, replicas)


def swap_cores(x):
    count = lax.axis_size("dp")
    return lax.ppermute(x, "dp", [(i, i ^ 1) for i in range(count)])


def swap_chips(x, mask_even, mask_odd):
    replicas = lax.axis_size("replica")
    pairs = []
    for dp in range(lax.axis_size("dp")):
        for z in range(replicas):
            chip = (dp // 2 * replicas + z) ^ (mask_odd if dp % 2 else mask_even)
            pairs.append((dp * replicas + z, (chip // replicas * 2 + dp % 2) * replicas + chip % replicas))
    return lax.ppermute(x, RANK_AXES, pairs)


def swap_tensor(x, mask):
    return lax.ppermute(x, "tensor", [(i, i ^ mask) for i in range(lax.axis_size("tensor"))])


def owners_of(row, chips, core, chip):
    half = chips - 2
    pairs = chip_masks(chips)
    mask = jnp.where(row < 2 * half + 2, SHARED, 0)
    for p, (even, odd) in enumerate(pairs):
        mine = jnp.where(core == 0, even, odd)
        theirs = jnp.where(core == 0, odd, even)
        mask = jnp.where(lax.div(row, 2) == p, mine, mask)
        mask = jnp.where(lax.div(row, 2) == p + len(pairs), theirs, mask)
    return rank_of(jnp.bitwise_xor(chip, mask), lax.rem(row, 2))


def halves(core, half, chunk, k):
    mine = pl.ds(pl.multiple_of(core * half + k * chunk, chunk), chunk)
    other = pl.ds(pl.multiple_of((1 - core) * half + k * chunk, chunk), chunk)
    return mine, other, pl.ds(k * chunk, chunk)


def owners_kernel(chips, out_ref):
    core, chip = where_am_i()
    out_ref[...] = owners_of(lax.broadcasted_iota(jnp.int32, out_ref.shape, 0), chips, core, chip)


def ordered(table_ref, owner_ref, features):
    pick = (table_ref[...] == owner_ref[...]).astype(f32)
    if pick.shape[0] <= 16:
        features = features.astype(f32)
        return sum(pick[:, j : j + 1] * features[j : j + 1] for j in range(pick.shape[0])).astype(bf16)
    pick = pick.astype(bf16)
    return jnp.dot(pick, features.astype(bf16), preferred_element_type=f32).astype(bf16)


def token_rows(depth, mask):
    shard = jnp.bitwise_xor(lax.axis_index("tensor"), mask)
    return pl.ds(pl.multiple_of(shard * depth, 32), depth)


def own_kernel(chunk, table_ref, owner_ref, feature_ref, g_ref, *refs):
    (total_ref,) = refs
    features = ordered(table_ref, owner_ref, feature_ref[...])
    held = token_rows(feature_ref.shape[1], 0)
    for k in range(total_ref.shape[1] // chunk):
        columns = pl.ds(k * chunk, chunk)
        total_ref[:, columns] = jnp.dot(features, g_ref[held, columns], preferred_element_type=f32)


def add_kernel(chunk, mask, table_ref, owner_ref, feature_ref, g_ref, before_ref, total_ref):
    features = ordered(table_ref, owner_ref, feature_ref[...])
    held = token_rows(feature_ref.shape[1], mask)
    for k in range(total_ref.shape[1] // chunk):
        columns = pl.ds(k * chunk, chunk)
        part = jnp.dot(features, g_ref[held, columns], preferred_element_type=f32)
        total_ref[:, columns] = before_ref[:, columns] + part


def last_kernel(chips, chunk, table_ref, owner_ref, feature_ref, g_ref, before_ref, *refs):
    own_refs, partner_refs, (keep_ref, send_ref, *state_refs) = refs[:3], refs[3:6], refs[6:]
    features = ordered(table_ref, owner_ref, feature_ref[...])
    held = token_rows(feature_ref.shape[1], 1)
    half = keep_ref.shape[1]
    served = chips - 2
    core, _ = where_am_i()
    for k in range(half // chunk):
        *sides, place = halves(core, half, chunk, k)
        mine, other = [
            (jnp.dot(features, g_ref[held, columns], preferred_element_type=f32) + before_ref[:, columns])
            .astype(bf16)
            .astype(f32)
            for columns in sides
        ]
        keep, send = [], []
        for p in range(0, served, 2):
            keep += [other[p : p + 2], mine[p : p + 2]]
            send += [mine[served + p : served + p + 2], other[served + p : served + p + 2]]
        keep_ref[:, place] = jnp.concatenate(keep + [mine[2 * served :]], axis=0)
        send_ref[:, place] = jnp.concatenate(send + [other[2 * served :]], axis=0).astype(bf16)
    for own_ref, partner_ref, ref in zip(own_refs, partner_refs, state_refs):
        own, partner = own_ref[...], partner_ref[...]
        ref[:1] = jnp.where(core == 0, own, partner)
        ref[1:] = jnp.where(core == 0, partner, own)


def corrections(step_ref):
    count = jnp.full((1, 128), step_ref[0], jnp.int32).astype(f32)
    first = 1.0 - jnp.exp(count * math.log(beta_first))
    second = 1.0 - jnp.exp(count * math.log(beta_second))
    return first[:, :1], second[:, :1]


def adam(gradient, master, first_moment, second_moment, correct_first, correct_second, rate):
    new_first = beta_first * first_moment + (1.0 - beta_first) * gradient
    new_second = beta_second * second_moment + (1.0 - beta_second) * gradient * gradient
    direction = new_first / correct_first / (jnp.sqrt(new_second / correct_second) + epsilon)
    new_master = master - rate * (direction + decay_rate * master)
    return new_master, new_first, new_second, direction


def chip_gradients(sums, others, tokens):
    return (sums[2:] + others[:2]) / tokens, (sums[:2] + others[2:]) / tokens


def params_kernel(chunk, tokens, step_ref, rate_ref, sums_ref, others_ref, *refs):
    state_refs, (params_ref, params_half_ref) = refs[:3], refs[3:]
    core, _ = where_am_i()
    corrected = corrections(step_ref)
    half = sums_ref.shape[1]
    for k in range(half // chunk):
        *sides, place = halves(core, half, chunk, k)
        values = []
        for columns, gradient in zip(sides, chip_gradients(sums_ref[:, place], others_ref[:, place], tokens)):
            state = [ref[:, columns] for ref in state_refs]
            values.append(adam(gradient, *state, *corrected, rate_ref[0])[0])
        params_ref[:, place] = jnp.concatenate(values[::-1], axis=0).astype(bf16)
        params_half_ref[:, place] = values[0].astype(bf16)


def state_kernel(chunk, tokens, step_ref, rate_ref, sums_ref, others_ref, *refs):
    state_refs, out_refs = refs[:3], refs[3:]
    core, _ = where_am_i()
    corrected = corrections(step_ref)
    half = sums_ref.shape[1]
    for k in range(half // chunk):
        *sides, place = halves(core, half, chunk, k)
        for columns, gradient in zip(sides, chip_gradients(sums_ref[:, place], others_ref[:, place], tokens)):
            gradient = jnp.where(core == 0, gradient[:1], gradient[1:])
            values = adam(gradient, *[ref[:, columns] for ref in state_refs], *corrected, rate_ref[0])
            for ref, value in zip(out_refs, values):
                ref[:, columns] = value


def picker(chips, rows, owner_ref, core, chip):
    column = lax.broadcasted_iota(jnp.int32, (rows, rows), 0)
    hot = (owners_of(column, chips, core, chip) == owner_ref[...]).astype(f32).T
    return hot.astype(bf16)


def early_kernel(chips, chunk, owner_ref, own_ref, half_ref, *refs):
    near_refs, (total_ref, mine_ref, other_ref) = refs[:-3], refs[-3:]
    core, chip = where_am_i()
    half = half_ref.shape[1]
    rows = total_ref.shape[0]
    served = chips - 2
    pick = picker(chips, rows, owner_ref, core, chip)
    own = pick[:, 2 * served + 2 :]
    shared = pick[:, 2 * served : 2 * served + 2]
    blank = jnp.zeros((rows, 2), f32)
    mine_columns, other_columns = [blank], [shared.astype(f32)]
    for p in range(served, 2 * served, 2):
        far = pick[:, p : p + 2].astype(f32)
        mine_columns += [far, blank]
        other_columns += [blank, far]
    mine_ref[...] = jnp.concatenate(mine_columns, axis=1).astype(bf16)
    other_ref[...] = jnp.concatenate(other_columns, axis=1).astype(bf16)
    for k in range(half // chunk):
        mine, other, place = halves(core, half, chunk, k)
        rows = own_ref[:, place].astype(f32)
        total = jnp.dot(shared, half_ref[:, place], preferred_element_type=f32)
        total += jnp.dot(own, rows[2:].astype(bf16), preferred_element_type=f32)
        total_other = jnp.dot(own, rows[:2].astype(bf16), preferred_element_type=f32)
        for p, near_ref in enumerate(near_refs):
            near = pick[:, 2 * p : 2 * p + 2]
            rows = near_ref[:, place].astype(f32)
            total += jnp.dot(near, rows[2:].astype(bf16), preferred_element_type=f32)
            total_other += jnp.dot(near, rows[:2].astype(bf16), preferred_element_type=f32)
        total_ref[:, mine] = total
        total_ref[:, other] = total_other


def order_kernel(chunk, mine_ref, other_ref, total_ref, far_ref, out_ref, rows_ref, sems):
    core, _ = where_am_i()
    half = far_ref.shape[1]
    copies = []
    for side, pick_ref in enumerate((mine_ref, other_ref)):
        pick = pick_ref[...]
        for k in range(half // chunk):
            *sides, place = halves(core, half, chunk, k)
            far = jnp.dot(pick, far_ref[:, place], preferred_element_type=f32)
            rows_ref[:, sides[side]] = (total_ref[:, sides[side]] + far).astype(bf16)
        done = halves(core, half, half, 0)[side]
        copies.append(pltpu.make_async_copy(rows_ref.at[:, done], out_ref.at[:, done], sems.at[side]))
        copies[side].start()
    for copy in copies:
        copy.wait()


VMEM = pl.BlockSpec(memory_space=pltpu.VMEM)
SMEM = pl.BlockSpec(memory_space=pltpu.SMEM)


def call(kernel, outs, specs, name, cost=None, out_spec=VMEM, scratch=()):
    return pl.pallas_call(
        kernel,
        out_shape=[jax.ShapeDtypeStruct(shape, dtype) for shape, dtype in outs],
        in_specs=specs,
        out_specs=[out_spec] * len(outs),
        scratch_shapes=scratch,
        compiler_params=pltpu.CompilerParams(vmem_limit_bytes=4 << 20),
        cost_estimate=cost,
        name=name,
    )


def on_device(
    features, output_grad, master, first_moment, second_moment, owner_map, step_count, learning_rate
):
    replicas = lax.axis_size("replica")
    chips = lax.axis_size("dp") // 2 * replicas
    _, tokens, columns = output_grad.shape
    rows = features.shape[2]
    ranks = owner_map.shape[0]
    half = columns // 2
    served = chips - 2
    chunk = 512 if half % 512 == 0 else 128
    pairs = chip_masks(chips)
    source = output_grad[0]
    owners = owner_map.reshape(1, ranks)

    mine = features[0].T
    diagonal, next_two, next_one = [swap_tensor(mine, mask) for mask in (3, 2, 1)]
    state = [x.reshape(1, columns) for x in (master, first_moment, second_moment)]
    (table,) = call(
        functools.partial(owners_kernel, chips),
        [((rows, rows), jnp.int32)],
        [],
        "owners",
        pl.CostEstimate(flops=3_000_000_000, bytes_accessed=0, transcendentals=0),
    )()
    total = ((rows, columns), f32)
    (part,) = call(functools.partial(own_kernel, chunk), [total], [VMEM] * 4, "own_tokens")(
        table, owners, mine, source
    )
    partner = [swap_cores(x) for x in state]
    for mask, block, name in ((3, diagonal, "diagonal_tokens"), (2, next_two, "next_two_tokens")):
        (part,) = call(functools.partial(add_kernel, chunk, mask), [total], [VMEM] * 5, name)(
            table, owners, block, source, part
        )
    keep, send, *state_rows = call(
        functools.partial(last_kernel, chips, chunk),
        [((2 * served + 4, half), f32), ((2 * served + 4, half), bf16)] + [((2, columns), f32)] * 3,
        [VMEM] * 11,
        "last_tokens",
    )(table, owners, next_one, source, part, *state, *partner)

    sums = keep + swap_cores(send).astype(f32)
    arrived = [swap_chips(sums[4 * p : 4 * p + 4].astype(bf16), *pair) for p, pair in enumerate(pairs)]
    arrived_half = swap_chips(sums[2 * served : 2 * served + 2].astype(bf16), SHARED, SHARED)
    sums_half = arrived_half.astype(f32) + sums[2 * served + 2 :]
    arrived = sum(x.astype(f32) for x in arrived)
    chip_sums = jnp.concatenate([arrived[:2], arrived[2:] + sums_half], axis=0)
    grads = (chip_sums, swap_cores(chip_sums))

    count = float(tokens * ranks)
    params, params_half = call(
        functools.partial(params_kernel, chunk, count),
        [((4, half), bf16), ((2, half), bf16)],
        [SMEM, SMEM] + [VMEM] * 5,
        "chip_params",
    )(step_count, learning_rate, *grads, *state_rows)
    outs = call(
        functools.partial(state_kernel, chunk, count),
        [((1, columns), f32)] * 4,
        [SMEM, SMEM] + [VMEM] * 5,
        "own_state",
    )(step_count, learning_rate, *grads, *state)
    near = [swap_chips(params, *pair) for pair in pairs]
    near_half = swap_chips(params_half, SHARED, SHARED)
    far = swap_cores(jnp.concatenate([near_half, *near], axis=0))
    early, *picks = call(
        functools.partial(early_kernel, chips, chunk),
        [total] + [((rows, 2 * served + 2), bf16)] * 2,
        [VMEM] * (3 + len(near)),
        "early_rows",
        pl.CostEstimate(flops=5_000_000_000, bytes_accessed=0, transcendentals=0),
    )(owners, params, near_half, *near)
    (params,) = call(
        functools.partial(order_kernel, chunk),
        [((rows, columns), bf16)],
        [VMEM] * 4,
        "row_order",
        out_spec=pl.BlockSpec(memory_space=pl.ANY),
        scratch=[pltpu.VMEM((rows, columns), bf16), pltpu.SemaphoreType.DMA((2,))],
    )(*picks, early, far)
    return (params, *[x.reshape(master.shape) for x in outs])


def solution(mesh):
    in_specs = (
        P(("dp", "replica"), "tensor", None),
        P(("dp", "replica"), None, "tensor"),
        P(("dp", "replica"), None, "tensor"),
        P(("dp", "replica"), None, "tensor"),
        P(("dp", "replica"), None, "tensor"),
        P(),
        P(),
        P(),
    )
    out_specs = (
        P(None, "tensor"),
        P(("dp", "replica"), None, "tensor"),
        P(("dp", "replica"), None, "tensor"),
        P(("dp", "replica"), None, "tensor"),
        P(("dp", "replica"), None, "tensor"),
    )
    return jax.shard_map(
        on_device, mesh=mesh, in_specs=in_specs, out_specs=out_specs, check_vma=False
    )
```

```python
import functools
import math
import jax
import jax.numpy as jnp
from jax import lax
from jax.experimental import pallas as pl
from jax.experimental.pallas import tpu as pltpu
from jax.sharding import PartitionSpec as P

beta_first = 0.9
beta_second = 0.95
epsilon = 1e-08
decay_rate = 0.1
f32, bf16 = jnp.float32, jnp.bfloat16
RANK_AXES = ("dp", "replica")


def chip_steps(chips):
    if chips == 4:
        return [(("shift", 1), ("mask", 2))], ("shift", 3)
    rest = [("mask", m) for m in range(2, chips)]
    return [(rest[i], rest[i + 1]) for i in range(0, len(rest), 2)], ("mask", 1)


def hop(chip, step, chips, back=False):
    kind, amount = step
    if kind == "mask":
        return chip ^ amount if isinstance(chip, int) else jnp.bitwise_xor(chip, amount)
    amount = chips - amount if back else amount
    return (chip + amount) % chips if isinstance(chip, int) else lax.rem(chip + amount, chips)


def where_am_i():
    replicas = lax.axis_size("replica")
    dp = lax.axis_index("dp")
    core = lax.rem(dp, 2)
    chip = lax.div(dp, 2) * replicas + lax.axis_index("replica")
    return core, chip


def rank_of(chip, core):
    replicas = lax.axis_size("replica")
    return (lax.div(chip, replicas) * 2 + core) * replicas + lax.rem(chip, replicas)


def swap_cores(x):
    count = lax.axis_size("dp")
    return lax.ppermute(x, "dp", [(i, i ^ 1) for i in range(count)])


def swap_chips(x, even, odd):
    replicas, count = lax.axis_size("replica"), lax.axis_size("dp")
    pairs = []
    for dp in range(count):
        for z in range(replicas):
            chip = hop(dp // 2 * replicas + z, odd if dp % 2 else even, count // 2 * replicas)
            pairs.append((dp * replicas + z, (chip // replicas * 2 + dp % 2) * replicas + chip % replicas))
    return lax.ppermute(x, RANK_AXES, pairs)


def swap_tensor(x, mask):
    return lax.ppermute(x, "tensor", [(i, i ^ mask) for i in range(lax.axis_size("tensor"))])


def owners_of(row, chips, core, chip, back=False):
    pairs, shared = chip_steps(chips)
    target = jnp.where(row < 4 * len(pairs) + 2, hop(chip, shared, chips, back), chip)
    for p, pair in enumerate(pairs):
        even, odd = [hop(chip, step, chips, back) for step in pair]
        target = jnp.where(lax.div(row, 2) == p, jnp.where(core == 0, even, odd), target)
        target = jnp.where(lax.div(row, 2) == p + len(pairs), jnp.where(core == 0, odd, even), target)
    return rank_of(target, lax.rem(row, 2))


def halves(core, half, chunk, k):
    mine = pl.ds(pl.multiple_of(core * half + k * chunk, chunk), chunk)
    other = pl.ds(pl.multiple_of((1 - core) * half + k * chunk, chunk), chunk)
    return mine, other, pl.ds(k * chunk, chunk)


def owners_kernel(chips, out_ref):
    core, chip = where_am_i()
    out_ref[...] = owners_of(lax.broadcasted_iota(jnp.int32, out_ref.shape, 0), chips, core, chip)


def ordered(table_ref, owner_ref, features):
    pick = (table_ref[...] == owner_ref[...]).astype(f32)
    if pick.shape[0] <= 16:
        features = features.astype(f32)
        return sum(pick[:, j : j + 1] * features[j : j + 1] for j in range(pick.shape[0])).astype(bf16)
    pick = pick.astype(bf16)
    return jnp.dot(pick, features.astype(bf16), preferred_element_type=f32).astype(bf16)


def token_rows(depth, mask):
    shard = jnp.bitwise_xor(lax.axis_index("tensor"), mask)
    return pl.ds(pl.multiple_of(shard * depth, 32), depth)


def own_kernel(chunk, table_ref, owner_ref, feature_ref, g_ref, *refs):
    (total_ref,) = refs
    features = ordered(table_ref, owner_ref, feature_ref[...])
    held = token_rows(feature_ref.shape[1], 0)
    for k in range(total_ref.shape[1] // chunk):
        columns = pl.ds(k * chunk, chunk)
        total_ref[:, columns] = jnp.dot(features, g_ref[held, columns], preferred_element_type=f32)


def add_kernel(chunk, mask, table_ref, owner_ref, feature_ref, g_ref, before_ref, total_ref):
    features = ordered(table_ref, owner_ref, feature_ref[...])
    held = token_rows(feature_ref.shape[1], mask)
    for k in range(total_ref.shape[1] // chunk):
        columns = pl.ds(k * chunk, chunk)
        part = jnp.dot(features, g_ref[held, columns], preferred_element_type=f32)
        total_ref[:, columns] = before_ref[:, columns] + part


def last_kernel(chips, chunk, table_ref, owner_ref, feature_ref, g_ref, before_ref, *refs):
    own_refs, partner_refs, (keep_ref, send_ref, *state_refs) = refs[:3], refs[3:6], refs[6:]
    features = ordered(table_ref, owner_ref, feature_ref[...])
    held = token_rows(feature_ref.shape[1], 1)
    half = keep_ref.shape[1]
    served = chips - 2
    core, _ = where_am_i()
    for k in range(half // chunk):
        *sides, place = halves(core, half, chunk, k)
        mine, other = [
            (jnp.dot(features, g_ref[held, columns], preferred_element_type=f32) + before_ref[:, columns])
            .astype(bf16)
            .astype(f32)
            for columns in sides
        ]
        keep, send = [], []
        for p in range(0, served, 2):
            keep += [other[p : p + 2], mine[p : p + 2]]
            send += [mine[served + p : served + p + 2], other[served + p : served + p + 2]]
        keep_ref[:, place] = jnp.concatenate(keep + [mine[2 * served :]], axis=0)
        send_ref[:, place] = jnp.concatenate(send + [other[2 * served :]], axis=0).astype(bf16)
    for own_ref, partner_ref, ref in zip(own_refs, partner_refs, state_refs):
        own, partner = own_ref[...], partner_ref[...]
        ref[:1] = jnp.where(core == 0, own, partner)
        ref[1:] = jnp.where(core == 0, partner, own)


def corrections(step_ref):
    count = jnp.full((1, 128), step_ref[0], jnp.int32).astype(f32)
    first = 1.0 - jnp.exp(count * math.log(beta_first))
    second = 1.0 - jnp.exp(count * math.log(beta_second))
    return first[:, :1], second[:, :1]


def adam(gradient, master, first_moment, second_moment, correct_first, correct_second, rate):
    new_first = beta_first * first_moment + (1.0 - beta_first) * gradient
    new_second = beta_second * second_moment + (1.0 - beta_second) * gradient * gradient
    direction = new_first / correct_first / (jnp.sqrt(new_second / correct_second) + epsilon)
    new_master = master - rate * (direction + decay_rate * master)
    return new_master, new_first, new_second, direction


def chip_gradients(sums, others, tokens):
    return (sums[2:] + others[:2]) / tokens, (sums[:2] + others[2:]) / tokens


def params_kernel(chunk, tokens, step_ref, rate_ref, sums_ref, others_ref, *refs):
    state_refs, (params_ref, params_half_ref) = refs[:3], refs[3:]
    core, _ = where_am_i()
    corrected = corrections(step_ref)
    half = sums_ref.shape[1]
    for k in range(half // chunk):
        *sides, place = halves(core, half, chunk, k)
        values = []
        for columns, gradient in zip(sides, chip_gradients(sums_ref[:, place], others_ref[:, place], tokens)):
            state = [ref[:, columns] for ref in state_refs]
            values.append(adam(gradient, *state, *corrected, rate_ref[0])[0])
        params_ref[:, place] = jnp.concatenate(values[::-1], axis=0).astype(bf16)
        params_half_ref[:, place] = values[0].astype(bf16)


def state_kernel(chunk, tokens, step_ref, rate_ref, sums_ref, others_ref, *refs):
    state_refs, out_refs = refs[:3], refs[3:]
    core, _ = where_am_i()
    corrected = corrections(step_ref)
    half = sums_ref.shape[1]
    for k in range(half // chunk):
        *sides, place = halves(core, half, chunk, k)
        for columns, gradient in zip(sides, chip_gradients(sums_ref[:, place], others_ref[:, place], tokens)):
            gradient = jnp.where(core == 0, gradient[:1], gradient[1:])
            values = adam(gradient, *[ref[:, columns] for ref in state_refs], *corrected, rate_ref[0])
            for ref, value in zip(out_refs, values):
                ref[:, columns] = value


def picker(chips, rows, owner_ref, core, chip):
    column = lax.broadcasted_iota(jnp.int32, (rows, rows), 0)
    hot = (owners_of(column, chips, core, chip, True) == owner_ref[...]).astype(f32).T
    return hot.astype(bf16)


def early_kernel(chips, chunk, owner_ref, own_ref, half_ref, *refs):
    near_refs, (total_ref, mine_ref, other_ref) = refs[:-3], refs[-3:]
    core, chip = where_am_i()
    half = half_ref.shape[1]
    rows = total_ref.shape[0]
    served = chips - 2
    pick = picker(chips, rows, owner_ref, core, chip)
    own = pick[:, 2 * served + 2 :]
    shared = pick[:, 2 * served : 2 * served + 2]
    blank = jnp.zeros((rows, 2), f32)
    mine_columns, other_columns = [blank], [shared.astype(f32)]
    for p in range(served, 2 * served, 2):
        far = pick[:, p : p + 2].astype(f32)
        mine_columns += [far, blank]
        other_columns += [blank, far]
    mine_ref[...] = jnp.concatenate(mine_columns, axis=1).astype(bf16)
    other_ref[...] = jnp.concatenate(other_columns, axis=1).astype(bf16)
    for k in range(half // chunk):
        mine, other, place = halves(core, half, chunk, k)
        rows = own_ref[:, place].astype(f32)
        total = jnp.dot(shared, half_ref[:, place], preferred_element_type=f32)
        total += jnp.dot(own, rows[2:].astype(bf16), preferred_element_type=f32)
        total_other = jnp.dot(own, rows[:2].astype(bf16), preferred_element_type=f32)
        for p, near_ref in enumerate(near_refs):
            near = pick[:, 2 * p : 2 * p + 2]
            rows = near_ref[:, place].astype(f32)
            total += jnp.dot(near, rows[2:].astype(bf16), preferred_element_type=f32)
            total_other += jnp.dot(near, rows[:2].astype(bf16), preferred_element_type=f32)
        total_ref[:, mine] = total
        total_ref[:, other] = total_other


def order_kernel(chunk, mine_ref, other_ref, total_ref, far_ref, out_ref):
    core, _ = where_am_i()
    half = far_ref.shape[1]
    picks = mine_ref[...], other_ref[...]
    for k in range(half // chunk):
        *sides, place = halves(core, half, chunk, k)
        for pick, columns in zip(picks, sides):
            far = jnp.dot(pick, far_ref[:, place], preferred_element_type=f32)
            out_ref[:, columns] = (total_ref[:, columns] + far).astype(bf16)


VMEM = pl.BlockSpec(memory_space=pltpu.VMEM)
SMEM = pl.BlockSpec(memory_space=pltpu.SMEM)


def call(kernel, outs, specs, name, cost=None):
    return pl.pallas_call(
        kernel,
        out_shape=[jax.ShapeDtypeStruct(shape, dtype) for shape, dtype in outs],
        in_specs=specs,
        out_specs=[VMEM] * len(outs),
        compiler_params=pltpu.CompilerParams(vmem_limit_bytes=4 << 20),
        cost_estimate=cost,
        name=name,
    )


def on_device(
    features, output_grad, master, first_moment, second_moment, owner_map, step_count, learning_rate
):
    replicas = lax.axis_size("replica")
    chips = lax.axis_size("dp") // 2 * replicas
    _, tokens, columns = output_grad.shape
    rows = features.shape[2]
    ranks = owner_map.shape[0]
    half = columns // 2
    served = chips - 2
    chunk = 512 if half % 512 == 0 else 128
    pairs, shared = chip_steps(chips)
    source = output_grad[0]
    owners = owner_map.reshape(1, ranks)

    mine = features[0].T
    diagonal, next_two, next_one = [swap_tensor(mine, mask) for mask in (3, 2, 1)]
    state = [x.reshape(1, columns) for x in (master, first_moment, second_moment)]
    (table,) = call(
        functools.partial(owners_kernel, chips),
        [((rows, rows), jnp.int32)],
        [],
        "owners",
        pl.CostEstimate(flops=3_000_000_000, bytes_accessed=0, transcendentals=0),
    )()
    total = ((rows, columns), f32)
    (part,) = call(functools.partial(own_kernel, chunk), [total], [VMEM] * 4, "own_tokens")(
        table, owners, mine, source
    )
    partner = [swap_cores(x) for x in state]
    for mask, block, name in ((3, diagonal, "diagonal_tokens"), (2, next_two, "next_two_tokens")):
        (part,) = call(functools.partial(add_kernel, chunk, mask), [total], [VMEM] * 5, name)(
            table, owners, block, source, part
        )
    keep, send, *state_rows = call(
        functools.partial(last_kernel, chips, chunk),
        [((2 * served + 4, half), f32), ((2 * served + 4, half), bf16)] + [((2, columns), f32)] * 3,
        [VMEM] * 11,
        "last_tokens",
    )(table, owners, next_one, source, part, *state, *partner)

    sums = keep + swap_cores(send).astype(f32)
    arrived = [swap_chips(sums[4 * p : 4 * p + 4].astype(bf16), *pair) for p, pair in enumerate(pairs)]
    arrived_half = swap_chips(sums[2 * served : 2 * served + 2].astype(bf16), shared, shared)
    sums_half = arrived_half.astype(f32) + sums[2 * served + 2 :]
    arrived = sum(x.astype(f32) for x in arrived)
    chip_sums = jnp.concatenate([arrived[:2], arrived[2:] + sums_half], axis=0)
    grads = (chip_sums, swap_cores(chip_sums))

    count = float(tokens * ranks)
    params, params_half = call(
        functools.partial(params_kernel, chunk, count),
        [((4, half), bf16), ((2, half), bf16)],
        [SMEM, SMEM] + [VMEM] * 5,
        "chip_params",
    )(step_count, learning_rate, *grads, *state_rows)
    outs = call(
        functools.partial(state_kernel, chunk, count),
        [((1, columns), f32)] * 4,
        [SMEM, SMEM] + [VMEM] * 5,
        "own_state",
    )(step_count, learning_rate, *grads, *state)
    near = [swap_chips(params, *pair) for pair in pairs]
    near_half = swap_chips(params_half, shared, shared)
    far = swap_cores(jnp.concatenate([near_half, *near], axis=0))
    early, *picks = call(
        functools.partial(early_kernel, chips, chunk),
        [total] + [((rows, 2 * served + 2), bf16)] * 2,
        [VMEM] * (3 + len(near)),
        "early_rows",
        pl.CostEstimate(flops=5_000_000_000, bytes_accessed=0, transcendentals=0),
    )(owners, params, near_half, *near)
    (params,) = call(
        functools.partial(order_kernel, chunk),
        [((rows, columns), bf16)],
        [VMEM] * 4,
        "row_order",
    )(*picks, early, far)
    return (params, *[x.reshape(master.shape) for x in outs])


def solution(mesh):
    in_specs = (
        P(("dp", "replica"), "tensor", None),
        P(("dp", "replica"), None, "tensor"),
        P(("dp", "replica"), None, "tensor"),
        P(("dp", "replica"), None, "tensor"),
        P(("dp", "replica"), None, "tensor"),
        P(),
        P(),
        P(),
    )
    out_specs = (
        P(None, "tensor"),
        P(("dp", "replica"), None, "tensor"),
        P(("dp", "replica"), None, "tensor"),
        P(("dp", "replica"), None, "tensor"),
        P(("dp", "replica"), None, "tensor"),
    )
    return jax.shard_map(
        on_device, mesh=mesh, in_specs=in_specs, out_specs=out_specs, check_vma=False
    )
```
